128 devices in a mesh: layer: 4 (over x_lo, core), fsdp: 32 (over x_hi, y, z).
Axes of the slice: x: 4 (x_hi: 2, x_lo: 2; x = x_hi * 2 + x_lo), y: 4, z: 4, core: 2. Of those that a mesh axis runs over, the one named last changes fastest.
Arguments:
- gradient: bfloat16 [4, 1536, 4608], P(None, ('layer', 'fsdp')), may hold values from -6 to 6
- eigenbasis: float32 [4, 4608, 4608], P('layer', 'fsdp'), may hold values from -0.09375 to 0.09375
- gram_sum: float32 [4, 4608, 4608], P('layer', 'fsdp'), may hold values from -6 to 6
- first_moment: float32 [4, 1536, 4608], P('layer', None, 'fsdp'), may hold values from -3 to 3
- second_moment: float32 [4, 1536, 4608], P('layer', None, 'fsdp'), may hold values from 0.1 to 4
Outputs:
- update: bfloat16 [4, 1536, 4608], P(None, ('layer', 'fsdp'))
- new_gram: float32 [4, 4608, 4608], P('layer', 'fsdp')
- new_first: float32 [4, 1536, 4608], P('layer', None, 'fsdp')
- new_second: float32 [4, 1536, 4608], P('layer', None, 'fsdp')
The draws below stay inside these ranges and needn't reach their ends.
All inputs are finite; a program needn't handle non-finite values.
Results may differ from the reference program's by a relative error of at most 0.0058.
Values may be sent and summed in bfloat16 or wider, within the bound.
No kernel may reach another device: no remote copies, remote signals or barrier semaphores. Data moves between devices by JAX's collectives and lax.ppermute only.
A program may use at most 192 MiB of HBM per device.

```python
import math
import jax
import jax.numpy as jnp
from jax import lax

D = 4608
LAYERS = 4
ROWS = 1536


def shard_levels(rng, extent, cuts, low, largest):
    factor_of = 1.0
    for dim, parts in cuts:
        steps = jax.random.uniform(jax.random.fold_in(jax.random.fold_in(rng, 6), dim), (parts,), jnp.float32, low / len(cuts), largest / len(cuts))
        factor_of = factor_of * jnp.repeat(jnp.exp(steps), extent[dim] // parts).reshape((-1,) + (1,) * (len(extent) - 1 - dim))
    return factor_of


def centred(own_key, shape, width, reach, shards=(), dtype=jnp.bfloat16):
    entries = jax.random.normal(own_key, shape, jnp.float32) * width
    if len(shards) > 0:
        entries = shard_levels(own_key, shape, shards, -0.22, 0.18) * entries
    return jnp.clip(entries, min=-reach, max=reach).astype(dtype)


def setup_inputs(seed: int = 0) -> dict:
    streams_of = jax.random.split(jax.random.key(seed), 6)
    return {
        "gradient": centred(streams_of[0], (LAYERS, ROWS, D), 1.0, 6.0, ((1, 128),)),
        "eigenbasis": centred(streams_of[1], (LAYERS, D, D), D ** -0.5, 0.09375, ((0, 4), (1, 32)), jnp.float32),
        "gram_sum": centred(streams_of[2], (LAYERS, D, D), 1.0, 6.0, ((0, 4), (1, 32)), jnp.float32),
        "first_moment": centred(streams_of[3], (LAYERS, ROWS, D), 0.5, 3.0, ((0, 4), (2, 32)), jnp.float32),
        "second_moment": jnp.clip(jnp.exp(math.log(4.0) - 3.6888794 * jax.random.uniform(streams_of[4], (LAYERS, ROWS, D), jnp.float32) ** shard_levels(streams_of[4], (LAYERS, ROWS, D), ((0, 4), (2, 32)), -0.2, 0.2)), 0.1, 4.0),
    }


bias_fix = 1.0 - 0.95 ** 10

def one_layer(grad_rows, basis_rows, gram_rows, first_rows, second_rows):
    grad_full = grad_rows.astype(jnp.float32)
    basis_half = lax.optimization_barrier(basis_rows.astype(jnp.bfloat16)).astype(jnp.float32)
    product = jnp.dot(grad_full.T, grad_full, precision=lax.Precision.HIGHEST)
    new_gram = 0.95 * gram_rows + 0.05 * product
    rotated = jnp.dot(grad_full, basis_half.T, precision=lax.Precision.HIGHEST)
    new_first = 0.95 * first_rows + 0.05 * rotated
    new_second = 0.95 * second_rows + 0.05 * rotated * rotated
    direction = new_first / bias_fix / (jnp.sqrt(new_second / bias_fix) + 1e-08)
    direction = lax.optimization_barrier(direction.astype(jnp.bfloat16)).astype(jnp.float32)
    update = jnp.dot(direction, basis_half, precision=lax.Precision.HIGHEST).astype(jnp.bfloat16)
    return (update, new_gram, new_first, new_second)

def reference(gradient, eigenbasis, gram_sum, first_moment, second_moment):
    results = [one_layer(gradient[index], eigenbasis[index], gram_sum[index], first_moment[index], second_moment[index]) for index in range(LAYERS)]
    update = jnp.stack([item[0] for item in results])
    new_gram = jnp.stack([item[1] for item in results])
    new_first = jnp.stack([item[2] for item in results])
    new_second = jnp.stack([item[3] for item in results])
    return (update, new_gram, new_first, new_second)
```

```python
import jax
import jax.numpy as jnp
from jax import lax
from jax.sharding import Mesh, PartitionSpec as P

bias_fix = 1.0 - 0.95**10
half = jnp.bfloat16
AXES = ("xl", "core", "xh", "y", "z")
OFFSETS = (0, -1, 1, 2)


def shift(value, axis, step):
    size = lax.axis_size(axis)
    return lax.ppermute(value, axis, [(i, (i + step) % size) for i in range(size)])


def shift_x(value, step):
    place = [(x % 2) * 2 + x // 2 for x in range(4)]
    return lax.ppermute(value, ("xl", "xh"), [(place[x], place[(x + step) % 4]) for x in range(4)])


def ring_gather(value, axis):
    cut = value.shape[0] // 2
    before = shift(value, axis, 1)
    after = shift(value, axis, -1)
    far_top = shift(before[:cut], axis, 1)
    far_low = shift(after[cut:], axis, -1)
    return jnp.concatenate([value, before, after, far_top, far_low], 0)


def ring_sum(blocks, axis):
    mine, to_before, to_after, far = blocks
    cut = mine.shape[0] // 2
    far = far.astype(half)
    top = shift(far[:cut], axis, 1)
    low = shift(far[cut:], axis, -1)
    up = jnp.concatenate([to_after[:cut] + top.astype(jnp.float32), to_after[cut:]], 0)
    down = jnp.concatenate([to_before[:cut], to_before[cut:] + low.astype(jnp.float32)], 0)
    up = shift(up.astype(half), axis, 1)
    down = shift(down.astype(half), axis, -1)
    return mine + up.astype(jnp.float32) + down.astype(jnp.float32)


def body(gradient, eigenbasis, gram_sum, first_moment, second_moment):
    rows = gradient.shape[1]
    width = gradient.shape[2]
    span = eigenbasis.shape[1]
    total = first_moment.shape[1]
    xl, core, xh, y, z = (lax.axis_index(a) for a in AXES)

    def pick(pair, index):
        return jnp.where(index == 0, pair[0], pair[1])

    pairs = gradient.reshape(2, 2, rows, width)
    keep = pick((pairs[:, 0], pairs[:, 1]), core)
    other = shift(pick((pairs[:, 1], pairs[:, 0]), core), "core", 1)
    chip = jnp.concatenate([keep, other], 1)
    own_layer = pick((chip[0], chip[1]), xl)
    next_layer = pick((chip[1], chip[0]), xl)
    line = jnp.concatenate(
        [own_layer, shift_x(next_layer, 1), shift_x(next_layer, -1), shift(own_layer, "xh", 1)], 0
    )
    grads = ring_gather(line, "y")
    count = grads.shape[0]

    basis = ring_gather(eigenbasis[0].astype(half), "z")

    at = lax.broadcasted_iota(jnp.int32, (1, 4 * count), 1)

    def offset(index):
        return jnp.where(index == 0, 0, jnp.where(index == 1, -1, index - 1))

    row = at % rows
    core_of = (core + at // rows) % 2
    x_of = (2 * xh + xl + offset(at // (2 * rows) % 4) + 4) % 4
    y_of = (y + offset(at // (8 * rows) % 4) + 4) % 4
    z_of = (z + offset(at // (32 * rows)) + 4) % 4
    number = ((((x_of % 2 * 2 + core_of) * 2 + x_of // 2) * 4 + y_of) * 4 + z_of) * rows + row
    order = (lax.broadcasted_iota(jnp.int32, (total, 4 * count), 0) == number).astype(half)

    first = first_moment[0].T
    second = second_moment[0].T
    first_high = first.astype(half)
    first_low = (first - first_high.astype(jnp.float32)).astype(half)
    moments = jnp.concatenate([first_high, first_low, second.astype(half)], 0)
    moments = jnp.dot(moments, order, preferred_element_type=jnp.float32).astype(half)
    moments = moments.reshape(3, span, 4, count)
    moved = [moments[:, :, 0]]
    for k, step in ((1, 1), (2, -1), (3, 2)):
        moved.append(shift(moments[:, :, (0, 2, 1, 3)[k]], "z", step))
    moved = jnp.concatenate(moved, 1).astype(jnp.float32)

    rotated = lax.dot_general(
        basis, grads, (((1,), (1,)), ((), ())), preferred_element_type=jnp.float32
    )
    new_first = 0.95 * (moved[0] + moved[1]) + 0.05 * rotated
    new_second = 0.95 * moved[2] + 0.05 * rotated * rotated
    direction = (new_first / bias_fix / (jnp.sqrt(new_second / bias_fix) + 1e-08)).astype(half)

    step_rows = count // 4
    terms = [
        lax.dot_general(
            direction[:, k * step_rows : (k + 1) * step_rows],
            basis,
            (((0,), (0,)), ((), ())),
            preferred_element_type=jnp.float32,
        )
        for k in range(4)
    ]
    summed = ring_sum(terms, "y").reshape(4, 2 * rows, width)
    sent = summed.astype(half)
    far = shift(sent[3], "xh", 1)
    left = shift_x(sent[1], -1)
    right = shift_x(sent[2], 1)
    own_update = (summed[0] + far.astype(jnp.float32)).astype(half)
    next_update = (left.astype(jnp.float32) + right.astype(jnp.float32)).astype(half)
    update = jnp.stack([pick((own_update, next_update), xl), pick((next_update, own_update), xl)])
    given = shift(update[:, rows:], "core", 1)
    update = update[:, :rows]
    update = jnp.stack([pick((update, given), core), pick((given, update), core)], 1)
    update = update.reshape(4, rows, width)

    terms = []
    for k in range(4):
        column = ((xh * 4 + y) * 4 + (z + OFFSETS[k] + 4) % 4) * span
        columns = lax.dynamic_slice_in_dim(grads, column, span, 1)
        terms.append(
            lax.dot_general(
                columns, grads, (((0,), (0,)), ((), ())), preferred_element_type=jnp.float32
            )
        )
    new_gram = 0.95 * gram_sum[0] + 0.05 * ring_sum(terms, "z")

    blocks = rotated.astype(half).reshape(4, span, count)
    owned = [blocks[0]]
    for k, step in ((1, 1), (2, -1), (3, 2)):
        owned.append(shift(blocks[(0, 2, 1, 3)[k]], "z", step))
    owned = lax.dot_general(
        jnp.concatenate(owned, 1), order, (((1,), (1,)), ((), ())), preferred_element_type=jnp.float32
    )
    out_first = 0.95 * first + 0.05 * owned
    out_second = 0.95 * second + 0.05 * owned * owned
    return (update, new_gram[None], out_first.T[None], out_second.T[None])


def solution(mesh):
    fine = Mesh(mesh.devices.reshape(2, 2, 2, 4, 4), AXES)
    layer, fsdp = ("xl", "core"), ("xh", "y", "z")
    return jax.shard_map(
        body,
        mesh=fine,
        in_specs=(
            P(None, AXES, None),
            P(layer, fsdp, None),
            P(layer, fsdp, None),
            P(layer, None, fsdp),
            P(layer, None, fsdp),
        ),
        out_specs=(
            P(None, AXES, None),
            P(layer, fsdp, None),
            P(layer, None, fsdp),
            P(layer, None, fsdp),
        ),
        check_vma=False,
    )
```

```python
import jax
import jax.numpy as jnp
from jax import lax
from jax.sharding import Mesh, PartitionSpec as P

bias_fix = 1.0 - 0.95**10
half = jnp.bfloat16
AXES = ("xl", "core", "xh", "y", "z")
OFFSETS = (-1, 1, 2, 0)


def route(value, target):
    sizes = (2, 2, 2, 4, 4)
    pairs = []
    for source in range(128):
        at, rest = [], source
        for size in reversed(sizes):
            at.append(rest % size)
            rest //= size
        place = 0
        for to, size in zip(target(*reversed(at)), sizes):
            place = place * size + to % size
        pairs.append((source, place))
    return lax.ppermute(value, AXES, pairs)


def shift_core(value):
    return route(value, lambda xl, c, xh, y, z: (xl, 1 - c, xh, y, z))


def shift_x(value, step):
    return route(
        value,
        lambda xl, c, xh, y, z: ((xl + step) % 2, c, (2 * xh + xl + step) % 4 // 2, y, z),
    )


def shift_own(value, step):
    return route(
        value, lambda xl, c, xh, y, z: (xl, c, xh, y + step * c, z + step * (1 - c))
    )


def shift_row(value, step):
    return route(
        value, lambda xl, c, xh, y, z: (xl, c, xh, y + step * (1 - c), z + step * c)
    )


def ring_near(own, shift):
    cut = own.shape[0] // 2
    before, after = shift(own, 1), shift(own, -1)
    return before, after, before[:cut], after[cut:]


def ring_far(own, near, shift):
    before, after, top, low = near
    return jnp.concatenate([before, after, shift(top, 1), shift(low, -1), own], 0)


def ring_sum(term, size, shift, wait=None):
    cut = size // 2
    top = shift(term(2, 0, cut).astype(half), 1)
    low = shift(term(2, cut, size - cut).astype(half), -1)
    if wait is not None:
        top, low, wait = lax.optimization_barrier((top, low, wait))
    up = term(1, 0, size) + jnp.pad(top.astype(jnp.float32), ((0, size - cut), (0, 0)))
    down = term(0, 0, size) + jnp.pad(low.astype(jnp.float32), ((cut, 0), (0, 0)))
    up = shift(up.astype(half), 1)
    down = shift(down.astype(half), -1)
    return up, down, wait


def body(gradient, eigenbasis, gram_sum, first_moment, second_moment):
    rows = gradient.shape[1]
    width = gradient.shape[2]
    span = eigenbasis.shape[1]
    total = first_moment.shape[1]
    xl, core, xh, y, z = (lax.axis_index(a) for a in AXES)

    def pick(pair, index):
        return jnp.where(index == 0, pair[0], pair[1])

    pairs = gradient.reshape(2, 2, rows, width)
    keep = pick((pairs[:, 0], pairs[:, 1]), core)
    other = shift_core(pick((pairs[:, 1], pairs[:, 0]), core))
    chip = jnp.concatenate([keep, other], 1)
    own_layer = pick((chip[0], chip[1]), xl)
    next_layer = pick((chip[1], chip[0]), xl)
    line = jnp.concatenate(
        [shift_x(next_layer, 1), shift_x(next_layer, -1), shift_x(own_layer, 2), own_layer], 0
    )
    count = 4 * line.shape[0]

    own_basis = eigenbasis[0].astype(half)
    near = ring_near(own_basis, shift_own)
    line_near = ring_near(line, shift_row)

    at = lax.broadcasted_iota(jnp.int32, (1, 4 * count), 1)

    def offset(index):
        return jnp.where(index == 0, -1, jnp.where(index == 3, 0, index))

    row = at % rows
    core_of = (core + at // rows) % 2
    x_of = (2 * xh + xl + offset(at // (2 * rows) % 4) + 4) % 4
    along_row = offset(at // (8 * rows) % 4) + 4
    along_own = offset(at // (32 * rows)) + 4
    y_of = (y + jnp.where(core == 0, along_row, along_own)) % 4
    z_of = (z + jnp.where(core == 0, along_own, along_row)) % 4
    number = ((((x_of % 2 * 2 + core_of) * 2 + x_of // 2) * 4 + y_of) * 4 + z_of) * rows + row
    order = (lax.broadcasted_iota(jnp.int32, (total, 4 * count), 0) == number).astype(half)

    first = first_moment[0].T
    second = second_moment[0].T
    first_high = first.astype(half)
    first_low = (first - first_high.astype(jnp.float32)).astype(half)
    moments = jnp.concatenate([first_high, first_low, second.astype(half)], 0)
    moments = jnp.dot(moments, order, preferred_element_type=jnp.float32).astype(half)
    moments, *tied = lax.optimization_barrier((moments, *near[2:]))
    near = (*near[:2], *tied)
    moments = [moments[:, k * count : (k + 1) * count] for k in range(4)]
    moved = [
        shift_own(moments[1], 1),
        shift_own(moments[0], -1),
        shift_own(moments[2], 2),
        moments[3],
    ]
    moved = [value.reshape(3, span, count) for value in moved]
    moved = jnp.concatenate(moved, 1).astype(jnp.float32)

    basis = ring_far(own_basis, near, shift_own)
    grads = ring_far(line, line_near, shift_row)
    rotated = lax.dot_general(
        basis, grads, (((1,), (1,)), ((), ())), preferred_element_type=jnp.float32
    )
    new_first = 0.95 * (moved[0] + moved[1]) + 0.05 * rotated
    new_second = 0.95 * moved[2] + 0.05 * rotated * rotated
    direction = (new_first / bias_fix / (jnp.sqrt(new_second / bias_fix) + 1e-08)).astype(half)

    def update_term(place, start, size):
        at = place * 8 * rows + start
        return lax.dot_general(
            direction[:, at : at + size],
            basis,
            (((0,), (0,)), ((), ())),
            preferred_element_type=jnp.float32,
        )

    up, down, _ = ring_sum(update_term, 8 * rows, shift_row)
    summed = update_term(3, 0, 8 * rows) + up.astype(jnp.float32) + down.astype(jnp.float32)
    summed = summed.reshape(4, 2 * rows, width)
    sent = summed.astype(half)
    far = shift_x(sent[2], 2)
    left = shift_x(sent[0], -1)
    right = shift_x(sent[1], 1)
    own_update = (summed[3] + far.astype(jnp.float32)).astype(half)
    next_update = (left.astype(jnp.float32) + right.astype(jnp.float32)).astype(half)
    update = jnp.stack([pick((own_update, next_update), xl), pick((next_update, own_update), xl)])
    def gram_term(place, start, size):
        y_at = (y + OFFSETS[place] * core + 4) % 4
        z_at = (z + OFFSETS[place] * (1 - core) + 4) % 4
        column = ((xh * 4 + y_at) * 4 + z_at) * span + start
        columns = lax.dynamic_slice_in_dim(grads, column, size, 1)
        return lax.dot_general(
            columns, grads, (((0,), (0,)), ((), ())), preferred_element_type=jnp.float32
        )

    blocks = rotated.astype(half).reshape(4, span, count)
    up, down, blocks = ring_sum(gram_term, span, shift_own, blocks)
    update, up, down = lax.optimization_barrier((update, up, down))
    product = gram_term(3, 0, span) + up.astype(jnp.float32) + down.astype(jnp.float32)
    new_gram = 0.95 * gram_sum[0] + 0.05 * product

    given = shift_core(update[:, rows:])
    update = update[:, :rows]
    update = jnp.stack([pick((update, given), core), pick((given, update), core)], 1)
    update = update.reshape(4, rows, width)

    owned = [
        shift_own(blocks[1], 1),
        shift_own(blocks[0], -1),
        shift_own(blocks[2], 2),
        blocks[3],
    ]
    owned = lax.dot_general(
        jnp.concatenate(owned, 1), order, (((1,), (1,)), ((), ())), preferred_element_type=jnp.float32
    )
    out_first = 0.95 * first + 0.05 * owned
    out_second = 0.95 * second + 0.05 * owned * owned
    return (update, new_gram[None], out_first.T[None], out_second.T[None])


def solution(mesh):
    fine = Mesh(mesh.devices.reshape(2, 2, 2, 4, 4), AXES)
    layer, fsdp = ("xl", "core"), ("xh", "y", "z")
    return jax.shard_map(
        body,
        mesh=fine,
        in_specs=(
            P(None, AXES, None),
            P(layer, fsdp, None),
            P(layer, fsdp, None),
            P(layer, None, fsdp),
            P(layer, None, fsdp),
        ),
        out_specs=(
            P(None, AXES, None),
            P(layer, fsdp, None),
            P(layer, None, fsdp),
            P(layer, None, fsdp),
        ),
        check_vma=False,
    )
```

```python
import jax
import jax.numpy as jnp
from jax import lax
from jax.sharding import Mesh, PartitionSpec as P

bias_fix = 1.0 - 0.95**10
half = jnp.bfloat16
AXES = ("xl", "core", "xh", "y", "z")
OFFSETS = (-1, 1, 2, 0)


def route(value, target):
    sizes = (2, 2, 2, 4, 4)
    pairs = []
    for source in range(128):
        at, rest = [], source
        for size in reversed(sizes):
            at.append(rest % size)
            rest //= size
        place = 0
        for to, size in zip(target(*reversed(at)), sizes):
            place = place * size + to % size
        pairs.append((source, place))
    return lax.ppermute(value, AXES, pairs)


def shift_core(value):
    return route(value, lambda xl, c, xh, y, z: (xl, 1 - c, xh, y, z))


def shift_x(value, step):
    return route(
        value,
        lambda xl, c, xh, y, z: ((xl + step) % 2, c, (2 * xh + xl + step) % 4 // 2, y, z),
    )


def shift_own(value, step):
    return route(
        value, lambda xl, c, xh, y, z: (xl, c, xh, y + step * c, z + step * (1 - c))
    )


def shift_row(value, step):
    return route(
        value, lambda xl, c, xh, y, z: (xl, c, xh, y + step * (1 - c), z + step * c)
    )


def ring_near(own, shift):
    return shift(own, 1), shift(own, -1)


def ring_far(near, shift, riders=None):
    cut = near[0].shape[1] // 2
    up, down = near[0][:, :cut], near[1][:, cut:]
    if riders is None:
        return shift(up, 1), shift(down, -1)
    up = shift(jnp.concatenate([up, riders[1]], 1), 1)
    down = shift(jnp.concatenate([down, riders[0]], 1), -1)
    return up[:, :cut], down[:, :cut], up[:, cut:], down[:, cut:]


def joined(own, near, far):
    return jnp.concatenate([*near, jnp.concatenate(far, 1), own], 0)


def ring_sum(term, width, shift, riders=None):
    cut = width // 2
    up, down = term(2, 0, cut).astype(half), term(2, cut, width).astype(half)
    if riders is not None:
        up = jnp.concatenate([up, riders[1]], 1)
        down = jnp.concatenate([down, riders[0]], 1)
    top, low = shift(up, 1), shift(down, -1)
    up = term(1, 0, width) + jnp.pad(top[:, :cut].astype(jnp.float32), ((0, 0), (0, cut)))
    down = term(0, 0, width) + jnp.pad(low[:, :cut].astype(jnp.float32), ((0, 0), (cut, 0)))
    up = shift(up.astype(half), 1)
    down = shift(down.astype(half), -1)
    return up, down, (top[:, cut:], low[:, cut:])


def body(gradient, eigenbasis, gram_sum, first_moment, second_moment):
    rows = gradient.shape[1]
    width = gradient.shape[2]
    span = eigenbasis.shape[1]
    total = first_moment.shape[1]
    xl, core, xh, y, z = (lax.axis_index(a) for a in AXES)

    def pick(pair, index):
        return jnp.where(index == 0, pair[0], pair[1])

    pairs = gradient.reshape(2, 2, rows, width)
    keep = pick((pairs[:, 0], pairs[:, 1]), core)
    other = shift_core(pick((pairs[:, 1], pairs[:, 0]), core))
    chip = jnp.concatenate([keep, other], 1)
    own_layer = pick((chip[0], chip[1]), xl)
    next_layer = pick((chip[1], chip[0]), xl)
    own_layer, next_layer, old_first, old_second = lax.optimization_barrier(
        (own_layer, next_layer, first_moment[0], second_moment[0])
    )
    line = jnp.concatenate(
        [shift_x(next_layer, 1), shift_x(next_layer, -1), shift_x(own_layer, 2), own_layer], 0
    )
    count = 4 * line.shape[0]

    own_basis = eigenbasis[0].astype(half)
    near = ring_near(own_basis, shift_own)
    line_near = ring_near(line, shift_row)

    at = lax.broadcasted_iota(jnp.int32, (1, 4 * count), 1)

    def offset(index):
        return jnp.where(index == 0, -1, jnp.where(index == 3, 0, index))

    row = at % rows
    core_of = (core + at // rows) % 2
    x_of = (2 * xh + xl + offset(at // (2 * rows) % 4) + 4) % 4
    along_row = offset(at // (8 * rows) % 4) + 4
    along_own = offset(at // (32 * rows)) + 4
    y_of = (y + jnp.where(core == 0, along_row, along_own)) % 4
    z_of = (z + jnp.where(core == 0, along_own, along_row)) % 4
    number = ((((x_of % 2 * 2 + core_of) * 2 + x_of // 2) * 4 + y_of) * 4 + z_of) * rows + row
    order = (lax.broadcasted_iota(jnp.int32, (total, 4 * count), 0) == number).astype(half)

    first = first_moment[0].T
    second = second_moment[0].T
    old_first = old_first.T
    first_high = old_first.astype(half)
    first_low = (old_first - first_high.astype(jnp.float32)).astype(half)
    moments = jnp.concatenate([first_high, first_low, old_second.T.astype(half)], 0)
    moments = jnp.dot(moments, order, preferred_element_type=jnp.float32).astype(half)
    moments = moments.reshape(3, span, 4 * count)
    moments = [
        jnp.concatenate(list(moments[:, :, k * count : (k + 1) * count]), 1) for k in range(4)
    ]
    farthest, *near = lax.optimization_barrier((moments[2], *near))
    top, low, moved_before, moved_after = ring_far(near, shift_own, moments[:2])
    moved = [moved_before, moved_after, shift_own(farthest, 2), moments[3]]
    moved = jnp.concatenate(moved, 0).astype(jnp.float32)
    moved = [moved[:, k * count : (k + 1) * count] for k in range(3)]

    basis = joined(own_basis, near, (top, low))
    grads = joined(line, line_near, ring_far(line_near, shift_row))
    rotated = lax.dot_general(
        basis, grads, (((1,), (1,)), ((), ())), preferred_element_type=jnp.float32
    )
    new_first = 0.95 * (moved[0] + moved[1]) + 0.05 * rotated
    new_second = 0.95 * moved[2] + 0.05 * rotated * rotated
    direction = (new_first / bias_fix / (jnp.sqrt(new_second / bias_fix) + 1e-08)).astype(half)

    def update_term(place, first, last):
        at = place * 8 * rows
        return lax.dot_general(
            direction[:, at : at + 8 * rows],
            basis[:, first:last],
            (((0,), (0,)), ((), ())),
            preferred_element_type=jnp.float32,
        )

    up, down, _ = ring_sum(update_term, width, shift_row)
    summed = update_term(3, 0, width) + up.astype(jnp.float32) + down.astype(jnp.float32)
    summed = summed.reshape(4, 2 * rows, width)
    sent = summed.astype(half)
    far = shift_x(sent[2], 2)
    left = shift_x(sent[0], -1)
    right = shift_x(sent[1], 1)
    own_update = (summed[3] + far.astype(jnp.float32)).astype(half)
    next_update = (left.astype(jnp.float32) + right.astype(jnp.float32)).astype(half)
    update = jnp.stack([pick((own_update, next_update), xl), pick((next_update, own_update), xl)])
    def gram_term(place, first, last):
        y_at = (y + OFFSETS[place] * core + 4) % 4
        z_at = (z + OFFSETS[place] * (1 - core) + 4) % 4
        column = ((xh * 4 + y_at) * 4 + z_at) * span
        columns = lax.dynamic_slice_in_dim(grads, column, span, 1)
        return lax.dot_general(
            columns,
            grads[:, first:last],
            (((0,), (0,)), ((), ())),
            preferred_element_type=jnp.float32,
        )

    blocks = rotated.astype(half).reshape(4, span, count)
    up, down, (from_before, from_after) = ring_sum(gram_term, width, shift_own, blocks[:2])
    owned = [from_before, from_after, shift_own(blocks[2], 2), blocks[3]]
    update, up, down = lax.optimization_barrier((update, up, down))
    product = gram_term(3, 0, width) + up.astype(jnp.float32) + down.astype(jnp.float32)
    new_gram = 0.95 * gram_sum[0] + 0.05 * product

    given = shift_core(update[:, rows:])
    update = update[:, :rows]
    update = jnp.stack([pick((update, given), core), pick((given, update), core)], 1)
    update = update.reshape(4, rows, width)

    owned = lax.dot_general(
        jnp.concatenate(owned, 1), order, (((1,), (1,)), ((), ())), preferred_element_type=jnp.float32
    )
    out_first = 0.95 * first + 0.05 * owned
    out_second = 0.95 * second + 0.05 * owned * owned
    return (update, new_gram[None], out_first.T[None], out_second.T[None])


def solution(mesh):
    fine = Mesh(mesh.devices.reshape(2, 2, 2, 4, 4), AXES)
    layer, fsdp = ("xl", "core"), ("xh", "y", "z")
    return jax.shard_map(
        body,
        mesh=fine,
        in_specs=(
            P(None, AXES, None),
            P(layer, fsdp, None),
            P(layer, fsdp, None),
            P(layer, None, fsdp),
            P(layer, None, fsdp),
        ),
        out_specs=(
            P(None, AXES, None),
            P(layer, fsdp, None),
            P(layer, None, fsdp),
            P(layer, None, fsdp),
        ),
        check_vma=False,
    )
```

```python
import jax
import jax.numpy as jnp
from jax import lax
from jax.sharding import Mesh, PartitionSpec as P

bias_fix = 1.0 - 0.95**10
half = jnp.bfloat16
AXES = ("xl", "core", "xh", "y", "z")
OFFSETS = (-1, 1, 2, 0)


def route(value, target):
    sizes = (2, 2, 2, 4, 4)
    pairs = []
    for source in range(128):
        at, rest = [], source
        for size in reversed(sizes):
            at.append(rest % size)
            rest //= size
        place = 0
        for to, size in zip(target(*reversed(at)), sizes):
            place = place * size + to % size
        pairs.append((source, place))
    return lax.ppermute(value, AXES, pairs)


def shift_core(value):
    return route(value, lambda xl, c, xh, y, z: (xl, 1 - c, xh, y, z))


def shift_x(value, step):
    return route(
        value,
        lambda xl, c, xh, y, z: ((xl + step) % 2, c, (2 * xh + xl + step) % 4 // 2, y, z),
    )


def shift_own(value, step):
    return route(
        value, lambda xl, c, xh, y, z: (xl, c, xh, y + step * c, z + step * (1 - c))
    )


def shift_row(value, step):
    return route(
        value, lambda xl, c, xh, y, z: (xl, c, xh, y + step * (1 - c), z + step * c)
    )


def ring_near(own, shift):
    return shift(own, 1), shift(own, -1)


def ring_far(near, shift, riders=None):
    cut = near[0].shape[1] // 2
    up, down = near[0][:, :cut], near[1][:, cut:]
    if riders is None:
        return shift(up, 1), shift(down, -1)
    up = shift(jnp.concatenate([up, riders[1]], 1), 1)
    down = shift(jnp.concatenate([down, riders[0]], 1), -1)
    return up[:, :cut], down[:, :cut], up[:, cut:], down[:, cut:]


def joined(own, near, far):
    return jnp.concatenate([*near, jnp.concatenate(far, 1), own], 0)


def ring_sum(term, width, shift, riders=None):
    cut = width // 2
    up, down = term(2, 0, cut).astype(half), term(2, cut, width).astype(half)
    if riders is not None:
        up = jnp.concatenate([up, riders[1]], 1)
        down = jnp.concatenate([down, riders[0]], 1)
    top, low = shift(up, 1), shift(down, -1)
    up = term(1, 0, width) + jnp.pad(top[:, :cut].astype(jnp.float32), ((0, 0), (0, cut)))
    down = term(0, 0, width) + jnp.pad(low[:, :cut].astype(jnp.float32), ((0, 0), (cut, 0)))
    up = shift(up.astype(half), 1)
    down = shift(down.astype(half), -1)
    return up, down, (top[:, cut:], low[:, cut:])


def body(gradient, eigenbasis, gram_sum, first_moment, second_moment):
    rows = gradient.shape[1]
    width = gradient.shape[2]
    span = eigenbasis.shape[1]
    total = first_moment.shape[1]
    xl, core, xh, y, z = (lax.axis_index(a) for a in AXES)

    def pick(pair, index):
        return jnp.where(index == 0, pair[0], pair[1])

    pairs = gradient.reshape(2, 2, rows, width)
    keep = pick((pairs[:, 0], pairs[:, 1]), core)
    other = shift_core(pick((pairs[:, 1], pairs[:, 0]), core))
    chip = jnp.concatenate([keep, other], 1)
    own_layer = pick((chip[0], chip[1]), xl)
    next_layer = pick((chip[1], chip[0]), xl)
    own_layer, next_layer, old_first, old_second = lax.optimization_barrier(
        (own_layer, next_layer, first_moment[0], second_moment[0])
    )
    line = jnp.concatenate(
        [shift_x(next_layer, 1), shift_x(next_layer, -1), shift_x(own_layer, 2), own_layer], 0
    )
    count = 4 * line.shape[0]

    own_basis = eigenbasis[0].astype(half)
    near = ring_near(own_basis, shift_own)
    line_near = ring_near(line, shift_row)

    at = lax.broadcasted_iota(jnp.int32, (1, 4 * count), 1)

    def offset(index):
        return jnp.where(index == 0, -1, jnp.where(index == 3, 0, index))

    row = at % rows
    core_of = (core + at // rows) % 2
    x_of = (2 * xh + xl + offset(at // (2 * rows) % 4) + 4) % 4
    along_row = offset(at // (8 * rows) % 4) + 4
    along_own = offset(at // (32 * rows)) + 4
    y_of = (y + jnp.where(core == 0, along_row, along_own)) % 4
    z_of = (z + jnp.where(core == 0, along_own, along_row)) % 4
    number = ((((x_of % 2 * 2 + core_of) * 2 + x_of // 2) * 4 + y_of) * 4 + z_of) * rows + row
    order = (lax.broadcasted_iota(jnp.int32, (total, 4 * count), 0) == number).astype(half)

    first = first_moment[0].T
    second = second_moment[0].T
    old_first = old_first.T
    first_high = old_first.astype(half)
    first_low = (old_first - first_high.astype(jnp.float32)).astype(half)
    moments = jnp.concatenate([first_high, first_low, old_second.T.astype(half)], 0)
    moments = jnp.dot(moments, order, preferred_element_type=jnp.float32).astype(half)
    moments = moments.reshape(3, span, 4 * count)
    moments = [
        jnp.concatenate(list(moments[:, :, k * count : (k + 1) * count]), 1) for k in range(4)
    ]
    farthest, *near = lax.optimization_barrier((moments[2], *near))
    top, low, moved_before, moved_after = ring_far(near, shift_own, moments[:2])
    moved = [moved_before, moved_after, shift_own(farthest, 2), moments[3]]
    moved = jnp.concatenate(moved, 0).astype(jnp.float32)
    moved = [moved[:, k * count : (k + 1) * count] for k in range(3)]

    far = lax.optimization_barrier(jnp.concatenate([top, low], 1))
    basis = jnp.concatenate([*near, far, own_basis], 0)
    grads = joined(line, line_near, ring_far(line_near, shift_row))
    rotated = lax.dot_general(
        basis, grads, (((1,), (1,)), ((), ())), preferred_element_type=jnp.float32
    )
    new_first = 0.95 * (moved[0] + moved[1]) + 0.05 * rotated
    new_second = 0.95 * moved[2] + 0.05 * rotated * rotated
    direction = (new_first / bias_fix / (jnp.sqrt(new_second / bias_fix) + 1e-08)).astype(half)

    def update_term(place, first, last):
        at = place * 8 * rows
        return lax.dot_general(
            direction[:, at : at + 8 * rows],
            basis[:, first:last],
            (((0,), (0,)), ((), ())),
            preferred_element_type=jnp.float32,
        )

    up, down, _ = ring_sum(update_term, width, shift_row)
    summed = update_term(3, 0, width) + up.astype(jnp.float32) + down.astype(jnp.float32)
    summed = summed.reshape(4, 2 * rows, width)
    sent = summed.astype(half)
    far = shift_x(sent[2], 2)
    left = shift_x(sent[0], -1)
    right = shift_x(sent[1], 1)
    own_update = (summed[3] + far.astype(jnp.float32)).astype(half)
    next_update = (left.astype(jnp.float32) + right.astype(jnp.float32)).astype(half)
    update = jnp.stack([pick((own_update, next_update), xl), pick((next_update, own_update), xl)])
    def gram_term(place, first, last):
        y_at = (y + OFFSETS[place] * core + 4) % 4
        z_at = (z + OFFSETS[place] * (1 - core) + 4) % 4
        column = ((xh * 4 + y_at) * 4 + z_at) * span
        columns = lax.dynamic_slice_in_dim(grads, column, span, 1)
        return lax.dot_general(
            columns,
            grads[:, first:last],
            (((0,), (0,)), ((), ())),
            preferred_element_type=jnp.float32,
        )

    blocks = rotated.astype(half).reshape(4, span, count)
    up, down, (from_before, from_after) = ring_sum(gram_term, width, shift_own, blocks[:2])
    owned = [from_before, from_after, shift_own(blocks[2], 2), blocks[3]]
    update, up, down = lax.optimization_barrier((update, up, down))
    product = gram_term(3, 0, width) + up.astype(jnp.float32) + down.astype(jnp.float32)
    new_gram = 0.95 * gram_sum[0] + 0.05 * product

    given = shift_core(update[:, rows:])
    update = update[:, :rows]
    update = jnp.stack([pick((update, given), core), pick((given, update), core)], 1)
    update = update.reshape(4, rows, width)

    owned = lax.dot_general(
        jnp.concatenate(owned, 1), order, (((1,), (1,)), ((), ())), preferred_element_type=jnp.float32
    )
    out_first = 0.95 * first + 0.05 * owned
    out_second = 0.95 * second + 0.05 * owned * owned
    return (update, new_gram[None], out_first.T[None], out_second.T[None])


def solution(mesh):
    fine = Mesh(mesh.devices.reshape(2, 2, 2, 4, 4), AXES)
    layer, fsdp = ("xl", "core"), ("xh", "y", "z")
    return jax.shard_map(
        body,
        mesh=fine,
        in_specs=(
            P(None, AXES, None),
            P(layer, fsdp, None),
            P(layer, fsdp, None),
            P(layer, None, fsdp),
            P(layer, None, fsdp),
        ),
        out_specs=(
            P(None, AXES, None),
            P(layer, fsdp, None),
            P(layer, None, fsdp),
            P(layer, None, fsdp),
        ),
        check_vma=False,
    )
```

```python
import jax
import jax.numpy as jnp
from jax import lax
from jax.sharding import Mesh, PartitionSpec as P

bias_fix = 1.0 - 0.95**10
half = jnp.bfloat16
AXES = ("xl", "core", "xh", "y", "z")
OFFSETS = (-1, 1, 2, 0)


def route(value, target):
    sizes = (2, 2, 2, 4, 4)
    pairs = []
    for source in range(128):
        at, rest = [], source
        for size in reversed(sizes):
            at.append(rest % size)
            rest //= size
        place = 0
        for to, size in zip(target(*reversed(at)), sizes):
            place = place * size + to % size
        pairs.append((source, place))
    return lax.ppermute(value, AXES, pairs)


def shift_core(value):
    return route(value, lambda xl, c, xh, y, z: (xl, 1 - c, xh, y, z))


def shift_x(value, step):
    return route(
        value,
        lambda xl, c, xh, y, z: ((xl + step) % 2, c, (2 * xh + xl + step) % 4 // 2, y, z),
    )


def shift_own(value, step):
    return route(
        value, lambda xl, c, xh, y, z: (xl, c, xh, y + step * c, z + step * (1 - c))
    )


def shift_row(value, step):
    return route(
        value, lambda xl, c, xh, y, z: (xl, c, xh, y + step * (1 - c), z + step * c)
    )


def ring_near(own, shift):
    return shift(own, 1), shift(own, -1)


def ring_far(near, shift, riders=None):
    cut = near[0].shape[1] // 2
    up, down = near[0][:, :cut], near[1][:, cut:]
    if riders is None:
        return shift(up, 1), shift(down, -1)
    up = shift(jnp.concatenate([up, riders[1]], 1), 1)
    down = shift(jnp.concatenate([down, riders[0]], 1), -1)
    return up[:, :cut], down[:, :cut], up[:, cut:], down[:, cut:]


def joined(own, near, far):
    return jnp.concatenate([*near, jnp.concatenate(far, 1), own], 0)


def ring_sum(term, width, shift, riders=None, wait=None):
    cut = width // 2
    up, down = term(2, 0, cut).astype(half), term(2, cut, width).astype(half)
    if riders is not None:
        up = jnp.concatenate([up, riders[1]], 1)
        down = jnp.concatenate([down, riders[0]], 1)
    top, low = shift(up, 1), shift(down, -1)
    if wait is not None:
        top, low, wait = lax.optimization_barrier((top, low, wait))
    up = term(1, 0, width) + jnp.pad(top[:, :cut].astype(jnp.float32), ((0, 0), (0, cut)))
    down = term(0, 0, width) + jnp.pad(low[:, :cut].astype(jnp.float32), ((0, 0), (cut, 0)))
    up = shift(up.astype(half), 1)
    down = shift(down.astype(half), -1)
    return up, down, (top[:, cut:], low[:, cut:]), wait


def body(gradient, eigenbasis, gram_sum, first_moment, second_moment):
    rows = gradient.shape[1]
    width = gradient.shape[2]
    span = eigenbasis.shape[1]
    total = first_moment.shape[1]
    xl, core, xh, y, z = (lax.axis_index(a) for a in AXES)

    def pick(pair, index):
        return jnp.where(index == 0, pair[0], pair[1])

    pairs = gradient.reshape(2, 2, rows, width)
    keep = pick((pairs[:, 0], pairs[:, 1]), core)
    other = shift_core(pick((pairs[:, 1], pairs[:, 0]), core))
    chip = jnp.concatenate([keep, other], 1)
    own_layer = pick((chip[0], chip[1]), xl)
    next_layer = pick((chip[1], chip[0]), xl)
    own_layer, next_layer, old_first, old_second = lax.optimization_barrier(
        (own_layer, next_layer, first_moment[0], second_moment[0])
    )
    line = jnp.concatenate(
        [shift_x(next_layer, 1), shift_x(next_layer, -1), shift_x(own_layer, 2), own_layer], 0
    )
    count = 4 * line.shape[0]

    own_basis = eigenbasis[0].astype(half)
    near = ring_near(own_basis, shift_own)
    line_near = ring_near(line, shift_row)

    at = lax.broadcasted_iota(jnp.int32, (1, 4 * count), 1)

    def offset(index):
        return jnp.where(index == 0, -1, jnp.where(index == 3, 0, index))

    row = at % rows
    core_of = (core + at // rows) % 2
    x_of = (2 * xh + xl + offset(at // (2 * rows) % 4) + 4) % 4
    along_row = offset(at // (8 * rows) % 4) + 4
    along_own = offset(at // (32 * rows)) + 4
    y_of = (y + jnp.where(core == 0, along_row, along_own)) % 4
    z_of = (z + jnp.where(core == 0, along_own, along_row)) % 4
    number = ((((x_of % 2 * 2 + core_of) * 2 + x_of // 2) * 4 + y_of) * 4 + z_of) * rows + row
    order = (lax.broadcasted_iota(jnp.int32, (total, 4 * count), 0) == number).astype(half)

    first = first_moment[0].T
    second = second_moment[0].T
    old_first = old_first.T
    first_high = old_first.astype(half)
    first_low = (old_first - first_high.astype(jnp.float32)).astype(half)
    moments = jnp.concatenate([first_high, first_low, old_second.T.astype(half)], 0)
    moments = jnp.dot(moments, order, preferred_element_type=jnp.float32).astype(half)
    moments = moments.reshape(3, span, 4 * count)
    moments = [
        jnp.concatenate(list(moments[:, :, k * count : (k + 1) * count]), 1) for k in range(4)
    ]
    farthest, *near = lax.optimization_barrier((moments[2], *near))
    top, low, moved_before, moved_after = ring_far(near, shift_own, moments[:2])
    moved = [moved_before, moved_after, shift_own(farthest, 2), moments[3]]
    moved = jnp.concatenate(moved, 0).astype(jnp.float32)
    moved = [moved[:, k * count : (k + 1) * count] for k in range(3)]

    far = lax.optimization_barrier(jnp.concatenate([top, low], 1))
    basis = jnp.concatenate([*near, far, own_basis], 0)
    grads = joined(line, line_near, ring_far(line_near, shift_row))
    rotated = lax.dot_general(
        basis, grads, (((1,), (1,)), ((), ())), preferred_element_type=jnp.float32
    )
    new_first = 0.95 * (moved[0] + moved[1]) + 0.05 * rotated
    new_second = 0.95 * moved[2] + 0.05 * rotated * rotated
    direction = (new_first / bias_fix / (jnp.sqrt(new_second / bias_fix) + 1e-08)).astype(half)

    def update_term(place, first, last):
        at = place * 8 * rows
        return lax.dot_general(
            direction[:, at : at + 8 * rows],
            basis[:, first:last],
            (((0,), (0,)), ((), ())),
            preferred_element_type=jnp.float32,
        )

    up, down, *_ = ring_sum(update_term, width, shift_row)
    summed = update_term(3, 0, width) + up.astype(jnp.float32) + down.astype(jnp.float32)
    summed = summed.reshape(4, 2 * rows, width)
    sent = summed.astype(half)
    far = shift_x(sent[2], 2)
    left = shift_x(sent[0], -1)
    right = shift_x(sent[1], 1)
    own_update = (summed[3] + far.astype(jnp.float32)).astype(half)
    next_update = (left.astype(jnp.float32) + right.astype(jnp.float32)).astype(half)
    update = jnp.stack([pick((own_update, next_update), xl), pick((next_update, own_update), xl)])
    def gram_term(place, first, last):
        y_at = (y + OFFSETS[place] * core + 4) % 4
        z_at = (z + OFFSETS[place] * (1 - core) + 4) % 4
        column = ((xh * 4 + y_at) * 4 + z_at) * span
        columns = lax.dynamic_slice_in_dim(grads, column, span, 1)
        return lax.dot_general(
            columns,
            grads[:, first:last],
            (((0,), (0,)), ((), ())),
            preferred_element_type=jnp.float32,
        )

    blocks = rotated.astype(half).reshape(4, span, count)
    up, down, (from_before, from_after), farthest = ring_sum(
        gram_term, width, shift_own, blocks[:2], blocks[2]
    )
    owned = [from_before, from_after, shift_own(farthest, 2), blocks[3]]
    update, up, down = lax.optimization_barrier((update, up, down))
    product = gram_term(3, 0, width) + up.astype(jnp.float32) + down.astype(jnp.float32)
    new_gram = 0.95 * gram_sum[0] + 0.05 * product

    given = shift_core(update[:, rows:])
    update = update[:, :rows]
    update = jnp.stack([pick((update, given), core), pick((given, update), core)], 1)
    update = update.reshape(4, rows, width)

    owned = lax.dot_general(
        jnp.concatenate(owned, 1), order, (((1,), (1,)), ((), ())), preferred_element_type=jnp.float32
    )
    out_first = 0.95 * first + 0.05 * owned
    out_second = 0.95 * second + 0.05 * owned * owned
    return (update, new_gram[None], out_first.T[None], out_second.T[None])


def solution(mesh):
    fine = Mesh(mesh.devices.reshape(2, 2, 2, 4, 4), AXES)
    layer, fsdp = ("xl", "core"), ("xh", "y", "z")
    return jax.shard_map(
        body,
        mesh=fine,
        in_specs=(
            P(None, AXES, None),
            P(layer, fsdp, None),
            P(layer, fsdp, None),
            P(layer, None, fsdp),
            P(layer, None, fsdp),
        ),
        out_specs=(
            P(None, AXES, None),
            P(layer, fsdp, None),
            P(layer, None, fsdp),
            P(layer, None, fsdp),
        ),
        check_vma=False,
    )
```
